32 devices in a mesh: dp: 8 (over y, x, core), head: 4 (over z).
Axes of the slice: x: 2, y: 2, z: 4, core: 2. Of those that a mesh axis runs over, the one named last changes fastest.
Arguments:
- tokens: bfloat16 [8192, 8192], P('dp'), may hold values from -64 to 64
- w_query: bfloat16 [8192, 8192], P('dp', 'head'), may hold values from -0.0625 to 0.0625
- key_weight: bfloat16 [8192, 1024], P('dp', 'head'), may hold values from -0.0625 to 0.0625
- value_weight: bfloat16 [8192, 1024], P('dp', 'head'), may hold values from -0.0625 to 0.0625
- segment_ids: int32 [8192], P('dp'), may hold values from 0 to 27, as said below
Outputs:
- attended: bfloat16 [8192, 8192], P('dp', 'head')
The draws below stay inside these ranges and needn't reach their ends.
Inputs may be any that keep to these rules, and one draw needn't show every extreme that they name: `segment_ids`: within each sequence of 1024 tokens the numbers start at 0 and never fall.
All inputs are finite; a program needn't handle non-finite values.
Results may differ from the reference program's by a relative error of at most 0.01.
The reference program's roundings to bfloat16 on the way count: a program that leaves them out, or rounds other values in their place, can miss the bound.
Values may be sent and summed in bfloat16 or wider, within the bound.
No kernel may reach another device: no remote copies, remote signals or barrier semaphores. Data moves between devices by JAX's collectives and lax.ppermute only.
A program may use at most 128 MiB of HBM per device.

```python
import jax
import jax.numpy as jnp
from jax import lax

MODEL_WIDTH = 8192
QUERY_HEADS = 64
KEY_VALUE_HEADS = 8
HEAD_SIZE = 128
PACKED_TOKENS = 1024
TOKENS = 8192
N_DP = 8


def draw_tokens(key, part):
    values = jnp.clip(jax.random.normal(key, (TOKENS, MODEL_WIDTH), jnp.float32), -6.0, 6.0)
    return values.astype(jnp.bfloat16)


def draw_segment_ids(key, part):
    first, second = jax.random.split(jax.random.fold_in(key, 11))
    level = jax.random.randint(first, (N_DP, 1), 0, 4)
    counts = level * level * level
    cuts = jax.random.randint(second, (N_DP, 27), 1, PACKED_TOKENS)
    active = jnp.arange(27)[None, :] < counts
    positions = jnp.arange(PACKED_TOKENS)
    passed = (cuts[:, None, :] <= positions[None, :, None]) & active[:, None, :]
    ids = jnp.sum(passed.astype(jnp.int32), axis=2).astype(jnp.int32)
    return ids.reshape(TOKENS)


def shard_levels(own_key, extent, cuts, least, top_value):
    def one(axis_at, blocks):
        heights = jax.random.uniform(jax.random.fold_in(jax.random.fold_in(own_key, 6), axis_at), (blocks,), jnp.float32, least / len(cuts), top_value / len(cuts))
        return jnp.repeat(jnp.exp(heights), extent[axis_at] // blocks).reshape((-1,) + (1,) * (len(extent) - axis_at - 1))

    loudness = one(*cuts[0])
    for cut in cuts[1:]:
        loudness = loudness * one(*cut)
    return loudness


def normal_values(rng, extent, width, most, cuts=(), kind=jnp.bfloat16):
    values = jax.random.normal(rng, extent, jnp.float32) * width
    if len(cuts) > 0:
        values = shard_levels(rng, extent, cuts, -0.22, 0.18) * values
    return jnp.clip(values, min=-most, max=most).astype(kind)


def setup_inputs(seed: int = 0) -> dict:
    seeds = jax.random.split(jax.random.key(seed), 6)
    tokens = draw_tokens(jax.random.fold_in(seeds[5], 71), 0)
    w_query = normal_values(seeds[1], (MODEL_WIDTH, QUERY_HEADS * HEAD_SIZE), MODEL_WIDTH ** -0.5, 0.0625, ((0, 8), (1, 4)))
    key_weight = normal_values(seeds[2], (MODEL_WIDTH, KEY_VALUE_HEADS * HEAD_SIZE), MODEL_WIDTH ** -0.5, 0.0625, ((0, 8), (1, 4)))
    value_weight = normal_values(seeds[3], (MODEL_WIDTH, KEY_VALUE_HEADS * HEAD_SIZE), MODEL_WIDTH ** -0.5, 0.0625, ((0, 8), (1, 4)))
    segment_ids = draw_segment_ids(jax.random.fold_in(seeds[5], 71), 0)
    return {"tokens": tokens, "w_query": w_query, "key_weight": key_weight, "value_weight": value_weight, "segment_ids": segment_ids}


def reference(tokens, w_query, key_weight, value_weight, segment_ids):
    grouped_heads = QUERY_HEADS // KEY_VALUE_HEADS

    def one_sequence(index):
        rows = lax.dynamic_slice_in_dim(tokens, index * PACKED_TOKENS, PACKED_TOKENS, 0)
        segments = lax.dynamic_slice_in_dim(segment_ids, index * PACKED_TOKENS, PACKED_TOKENS, 0)
        query_matrix = jnp.dot(rows, w_query, preferred_element_type=jnp.float32).astype(jnp.bfloat16)
        key = jnp.dot(rows, key_weight, preferred_element_type=jnp.float32).astype(jnp.bfloat16)
        value_matrix = jnp.dot(rows, value_weight, preferred_element_type=jnp.float32).astype(jnp.bfloat16)
        query_matrix = query_matrix.reshape(PACKED_TOKENS, KEY_VALUE_HEADS, grouped_heads, HEAD_SIZE).astype(jnp.float32)
        key = key.reshape(PACKED_TOKENS, KEY_VALUE_HEADS, HEAD_SIZE).astype(jnp.float32)
        value_matrix = value_matrix.reshape(PACKED_TOKENS, KEY_VALUE_HEADS, HEAD_SIZE).astype(jnp.float32)
        positions = jnp.arange(PACKED_TOKENS, dtype=jnp.int32)
        mask = (positions[None, :] <= positions[:, None]) & (segments[None, :] == segments[:, None])
        scores = jnp.einsum('qhgd,khd->hgqk', query_matrix, key) / jnp.sqrt(jnp.float32(HEAD_SIZE))
        scores = jnp.where(mask, scores, jnp.float32(-1e+30))
        highest = lax.optimization_barrier(jnp.max(scores, axis=3, keepdims=True))
        weights = jnp.where(mask, jnp.exp(scores - highest), jnp.float32(0.0))
        denominator = lax.optimization_barrier(jnp.sum(weights, axis=3))
        rounded = lax.optimization_barrier(weights.astype(jnp.bfloat16)).astype(jnp.float32)
        summed = jnp.einsum('hgqk,khd->hgqd', rounded, value_matrix)
        result = summed / denominator[..., None]
        return jnp.transpose(result, (2, 0, 1, 3)).reshape(PACKED_TOKENS, QUERY_HEADS * HEAD_SIZE).astype(jnp.bfloat16)
    outputs = lax.map(one_sequence, jnp.arange(N_DP, dtype=jnp.int32))
    return outputs.reshape(TOKENS, QUERY_HEADS * HEAD_SIZE)
```

```python
import functools
import math

import jax
import jax.numpy as jnp
from jax import lax
from jax.experimental import pallas as pl
from jax.experimental.pallas import tpu as pltpu
from jax.sharding import PartitionSpec as P

QUERY_HEADS = 64
KEY_VALUE_HEADS = 8
HEAD_SIZE = 128
GROUP = QUERY_HEADS // KEY_VALUE_HEADS
CHUNK = 256
ROW_BLOCK = 256
NEGATIVE = -1e30
VMEM_BYTES = 56 * 1024 * 1024


def ring_of(n_dp):
    chips = n_dp // 2
    half = chips // 2
    return list(range(half)) + list(range(chips - 1, half - 1, -1))


def shift_pairs(n_dp, step):
    ring = ring_of(n_dp)
    size = len(ring)
    return [
        (ring[at] * 2 + core, ring[(at + step) % size] * 2 + core)
        for at in range(size)
        for core in range(2)
    ]


def attend_rows(query, keys, values, allowed):
    scale = math.log2(math.e) / math.sqrt(HEAD_SIZE)
    scores = lax.dot_general(query, keys, (((1,), (1,)), ((), ())), preferred_element_type=jnp.float32)
    scores = jnp.where(allowed, scores, NEGATIVE)
    top = jnp.max(scores, axis=1, keepdims=True)
    weights = jnp.exp2((scores - top) * scale)
    denominator = jnp.sum(weights, axis=1, keepdims=True)
    summed = jnp.dot(weights.astype(jnp.bfloat16), values, preferred_element_type=jnp.float32)
    return (summed / denominator).astype(jnp.bfloat16)


def attend_chunk(query, key_ref, value_ref, seg_row_ref, seg_col_ref, out_ref):
    rows = query.shape[0]
    heads = query.shape[1] // HEAD_SIZE
    for start in range(0, rows, ROW_BLOCK):
        stop = min(start + ROW_BLOCK, rows)
        seg_q = seg_col_ref[start:stop, :]
        seg_k = seg_row_ref[:, :stop]
        at_q = start + lax.broadcasted_iota(jnp.int32, (stop - start, stop), 0)
        at_k = lax.broadcasted_iota(jnp.int32, (stop - start, stop), 1)
        allowed = (seg_q == seg_k) & (at_k <= at_q)
        for head in range(heads):
            columns = slice(head * HEAD_SIZE, (head + 1) * HEAD_SIZE)
            out_ref[start:stop, columns] = attend_rows(
                query[start:stop, columns], key_ref[:stop, :], value_ref[:stop, :], allowed
            )


def project_kernel(n_pieces, has_start, mode, order_ref, tokens_ref, *refs):
    pieces = refs[:n_pieces]
    refs = refs[n_pieces:]
    start_ref = None
    if has_start:
        start_ref, refs = refs[0], refs[1:]
    if mode == "attend":
        key_ref, value_ref, seg_row_ref, seg_col_ref = refs[:4]
        out_ref, total = refs[-2:]
    elif mode == "partial":
        (out_ref,) = refs
        total = out_ref
    else:
        out_ref, total = refs
    step = pl.program_id(0)
    for at, piece in enumerate(pieces):

        @pl.when(step == at)
        def _(at=at, piece=piece):
            part = jnp.dot(tokens_ref[...], piece[...], preferred_element_type=jnp.float32)
            if at > 0:
                part = part + total[...]
            elif has_start:
                part = part + start_ref[...]
            if at < n_pieces - 1 or mode == "partial":
                total[...] = part
            elif mode == "round":
                out_ref[...] = part.astype(jnp.bfloat16)
            else:
                attend_chunk(
                    part.astype(jnp.bfloat16), key_ref, value_ref, seg_row_ref, seg_col_ref, out_ref
                )


def project(tokens, order, pieces, width, mode, start=None, attention=None, name=None):
    rows = tokens.shape[0]
    depth = pieces[0][0].shape[0]
    n_pieces = len(pieces)
    whole = lambda step, order: (0, 0)
    in_specs = [pl.BlockSpec((rows, depth), lambda step, order: (0, order[step]))]
    args = [tokens]
    for array, block in pieces:
        in_specs.append(pl.BlockSpec((depth, width), lambda step, order, block=block: (0, block)))
        args.append(array)
    if start is not None:
        in_specs.append(pl.BlockSpec((rows, width), whole))
        args.append(start)
    scratch = [pltpu.VMEM((rows, width), jnp.float32)]
    aliases = {}
    flops = 2 * rows * depth * n_pieces * width
    if mode == "attend":
        keys, values, kv_block, seg_row, seg_col, out, column, out_columns = attention
        kv_spec = pl.BlockSpec((rows, HEAD_SIZE), lambda step, order: (0, kv_block))
        in_specs += [kv_spec, kv_spec, pl.BlockSpec(seg_row.shape, whole), pl.BlockSpec(seg_col.shape, whole)]
        args += [keys, values, seg_row, seg_col]
        if out is not None:
            in_specs.append(pl.BlockSpec(memory_space=pl.ANY))
            args.append(out)
            aliases = {len(args): 0}
        out_shape = jax.ShapeDtypeStruct((rows, out_columns), jnp.bfloat16)
        out_spec = pl.BlockSpec((rows, width), lambda step, order: (0, column))
        flops += 4 * rows * rows * width
    elif mode == "partial":
        scratch = []
        out_shape = jax.ShapeDtypeStruct((rows, width), jnp.float32)
        out_spec = pl.BlockSpec((rows, width), whole)
    else:
        out_shape = jax.ShapeDtypeStruct((rows, width), jnp.bfloat16)
        out_spec = pl.BlockSpec((rows, width), whole)
    return pl.pallas_call(
        functools.partial(project_kernel, n_pieces, start is not None, mode),
        grid_spec=pltpu.PrefetchScalarGridSpec(
            num_scalar_prefetch=1,
            grid=(n_pieces,),
            in_specs=in_specs,
            out_specs=out_spec,
            scratch_shapes=scratch,
        ),
        out_shape=out_shape,
        input_output_aliases=aliases,
        compiler_params=pltpu.CompilerParams(
            dimension_semantics=("arbitrary",), vmem_limit_bytes=VMEM_BYTES
        ),
        cost_estimate=pl.CostEstimate(
            flops=flops, bytes_accessed=2 * rows * depth * n_pieces, transcendentals=0
        ),
        name=name,
    )(order, *args)


def body(tokens, w_query, key_weight, value_weight, segment_ids):
    n_dp = lax.axis_size("dp")
    ring = ring_of(n_dp)
    size = len(ring)
    hops = size // 2
    right = functools.partial(lax.ppermute, axis_name="dp", perm=shift_pairs(n_dp, 1))
    left = functools.partial(lax.ppermute, axis_name="dp", perm=shift_pairs(n_dp, -1))
    sibling = functools.partial(lax.ppermute, axis_name="dp", perm=[(at, at ^ 1) for at in range(n_dp)])

    tables = {"whole": [], "split": [], "early": [], "late": []}
    for device in range(n_dp):
        at, core = ring.index(device // 2), device % 2
        near = [at]
        for hop in range(1, hops):
            near += [(at - hop) % size, (at + hop) % size]
        far = (at + hops) % size
        early = [ring[chip] * 2 + (core ^ other) for chip in near for other in range(2)]
        late = [ring[far] * 2 + (core ^ other) for other in range(2)]
        tables["early"].append(early)
        tables["whole"].append(early + late)
        tables["late"].append([late[0] * 2, late[0] * 2 + 1, late[1] * 2, late[1] * 2 + 1])
    me = lax.axis_index("dp")
    order = {
        kind: jnp.asarray(tables[kind], jnp.int32)[me] for kind in ("early", "whole", "late")
    }

    def gather(piece, mode):
        near = []
        from_left = from_right = piece
        for _ in range(1, hops):
            from_left, from_right = right(from_left), left(from_right)
            near += [from_left, sibling(from_left), from_right, sibling(from_right)]
        if mode == "right":
            far = [right(from_left)]
        elif mode == "left":
            far = [left(from_right)]
        else:
            middle = piece.shape[0] // 2
            far = [right(from_left[:middle]), left(from_right[middle:])]
        return near, far + [sibling(part) for part in far]

    key_sibling, value_sibling = sibling(key_weight), sibling(value_weight)
    key_near, key_far = gather(key_weight, "right")
    value_near, value_far = gather(value_weight, "left")
    query_sibling = sibling(w_query)

    def paired(arrays, block=0):
        return [(array, block) for array in arrays]

    kv_width = key_weight.shape[1]
    keys = project(
        tokens, order["whole"], paired([key_weight, key_sibling] + key_near + key_far), kv_width, "round", name="project_keys"
    )
    values = project(
        tokens, order["whole"], paired([value_weight, value_sibling] + value_near + value_far), kv_width, "round", name="project_values"
    )
    seg_row = segment_ids.reshape(1, -1)
    seg_col = segment_ids.reshape(-1, 1)

    columns = w_query.shape[1]
    out = None
    n_chunks = columns // CHUNK
    for chunk in range(n_chunks):
        mode = "split" if chunk >= n_chunks - 2 else ("right", "left")[chunk % 2]
        piece = w_query[:, chunk * CHUNK : (chunk + 1) * CHUNK]
        near, far = gather(piece, mode)
        local = paired([w_query, query_sibling], chunk) + paired(near)
        kv_block = chunk * CHUNK // (GROUP * HEAD_SIZE)
        attention = (keys, values, kv_block, seg_row, seg_col, out, chunk, columns)
        if mode == "split":
            start = project(tokens, order["early"], local, CHUNK, "partial", name="project_near")
            out = project(tokens, order["late"], paired(far), CHUNK, "attend", start, attention, name="project_far_attend")
        else:
            out = project(tokens, order["whole"], local + paired(far), CHUNK, "attend", None, attention, name="project_attend")
    return out


def solution(mesh):
    in_specs = (P("dp", None), P("dp", "head"), P("dp", "head"), P("dp", "head"), P("dp"))
    out_specs = P("dp", "head")
    return jax.shard_map(body, mesh=mesh, in_specs=in_specs, out_specs=out_specs, check_vma=False)
```

```python
import functools
import math

import jax
import jax.numpy as jnp
from jax import lax
from jax.experimental import pallas as pl
from jax.experimental.pallas import tpu as pltpu
from jax.sharding import PartitionSpec as P

QUERY_HEADS = 64
KEY_VALUE_HEADS = 8
HEAD_SIZE = 128
GROUP = QUERY_HEADS // KEY_VALUE_HEADS
ROW_BLOCK = 256
WIDE = 512
NARROW = 256
NEGATIVE = -1e30
VMEM_BYTES = 16 * 1024 * 1024


def ring_of(n_dp):
    chips = n_dp // 2
    half = chips // 2
    return list(range(half)) + list(range(chips - 1, half - 1, -1))


def ring_pairs(n_dp, step):
    ring = ring_of(n_dp)
    size = len(ring)
    return [
        (ring[at] * 2 + core, ring[(at + (step if core == 0 else -step)) % size] * 2 + core)
        for at in range(size)
        for core in range(2)
    ]


def attend_rows(query, keys, values, allowed):
    scale = math.log2(math.e) / math.sqrt(HEAD_SIZE)
    scores = lax.dot_general(query, keys, (((1,), (1,)), ((), ())), preferred_element_type=jnp.float32)
    scores = jnp.where(allowed, scores, NEGATIVE)
    top = jnp.max(scores, axis=1, keepdims=True)
    weights = jnp.exp2((scores - top) * scale).astype(jnp.bfloat16)
    values = jnp.concatenate([values, jnp.ones_like(values)], axis=1)
    summed = jnp.dot(weights, values, preferred_element_type=jnp.float32)
    return (summed[:, :HEAD_SIZE] / summed[:, HEAD_SIZE:]).astype(jnp.bfloat16)


def chunk_kernel(n_pieces, has_start, mode, kv_at, column, order_ref, tokens_ref, *refs):
    pieces, refs = refs[:n_pieces], refs[n_pieces:]
    rows = tokens_ref.shape[0]
    depth, width = pieces[0].shape
    total = None
    if has_start:
        total = refs[0][...]
        refs = refs[1:]
    for at, piece in enumerate(pieces):
        columns = pl.ds(pl.multiple_of(order_ref[at] * depth, depth), depth)
        part = jnp.dot(tokens_ref[:, columns], piece[...], preferred_element_type=jnp.float32)
        total = part if total is None else total + part
    if mode == "partial":
        refs[-2][...] = total
        refs[-1][...] = jnp.zeros_like(refs[-1])
        return
    if mode == "round":
        refs[-2][...] = total.astype(jnp.bfloat16)
        refs[-1][...] = jnp.zeros_like(refs[-1])
        return
    kv_ref, seg_row_ref, seg_col_ref = refs[:3]
    out_ref, done_ref, query_ref, block_ref, out_sems = refs[-5:]
    done_ref[...] = jnp.zeros_like(done_ref)
    query_ref[...] = total.astype(jnp.bfloat16)
    half = kv_ref.shape[1] // 2
    copies = []
    for number in range(rows // ROW_BLOCK):
        start, stop = number * ROW_BLOCK, (number + 1) * ROW_BLOCK
        at_q = start + lax.broadcasted_iota(jnp.int32, (ROW_BLOCK, stop), 0)
        at_k = lax.broadcasted_iota(jnp.int32, (ROW_BLOCK, stop), 1)
        allowed = (seg_col_ref[start:stop, :] == seg_row_ref[:, :stop]) & (at_k <= at_q)
        for head in range(0, width, HEAD_SIZE):
            block_ref[start:stop, head : head + HEAD_SIZE] = attend_rows(
                query_ref[start:stop, head : head + HEAD_SIZE],
                kv_ref[:stop, kv_at * HEAD_SIZE : (kv_at + 1) * HEAD_SIZE],
                kv_ref[:stop, half + kv_at * HEAD_SIZE : half + (kv_at + 1) * HEAD_SIZE],
                allowed,
            )
        block = pl.ds(start, ROW_BLOCK)
        copy = pltpu.make_async_copy(
            block_ref.at[block, :], out_ref.at[block, pl.ds(column, width)], out_sems.at[number]
        )
        copy.start()
        copies.append(copy)
    for copy in copies:
        copy.wait()


def chunk_call(tokens, order, pieces, mode, name, done, start=None, attention=None):
    rows, model = tokens.shape
    depth, width = pieces[0].shape
    in_hbm = pl.BlockSpec(memory_space=pltpu.HBM)
    in_vmem = pl.BlockSpec(memory_space=pltpu.VMEM)
    args = [order, tokens] + list(pieces)
    if start is not None:
        args.append(start)
    in_specs = [pl.BlockSpec(memory_space=pltpu.SMEM)] + [in_vmem] * (len(args) - 1)
    aliases = {}
    scratch = []
    flops = 2 * rows * depth * len(pieces) * width
    kv_at = column = 0
    out_spec = in_vmem
    out_shape = jax.ShapeDtypeStruct((rows, width), jnp.float32 if mode == "partial" else jnp.bfloat16)
    if mode == "attend":
        kv, kv_at, seg_row, seg_col, out, column, out_columns = attention
        args += [kv, seg_row, seg_col]
        in_specs += [in_vmem] * 3
        flops += 8 * rows * rows * width
        out_spec = in_hbm
        out_shape = jax.ShapeDtypeStruct((rows, out_columns), jnp.bfloat16)
        scratch = [
            pltpu.VMEM((rows, width), jnp.bfloat16),
            pltpu.VMEM((rows, width), jnp.bfloat16),
            pltpu.SemaphoreType.DMA((rows // ROW_BLOCK,)),
        ]
        if out is not None:
            aliases = {len(args): 0}
            in_specs.append(in_hbm)
            args.append(out)
    if done is not None:
        in_specs.append(in_vmem)
        args.append(done)
    return pl.pallas_call(
        functools.partial(chunk_kernel, len(pieces), start is not None, mode, kv_at, column),
        in_specs=in_specs,
        out_specs=(out_spec, in_vmem),
        out_shape=(out_shape, jax.ShapeDtypeStruct((8, 128), jnp.float32)),
        scratch_shapes=scratch,
        input_output_aliases=aliases,
        compiler_params=pltpu.CompilerParams(vmem_limit_bytes=VMEM_BYTES),
        cost_estimate=pl.CostEstimate(flops=flops, bytes_accessed=0, transcendentals=0),
        name=name,
    )(*args)


def hold(value, *others):
    return lax.optimization_barrier((value,) + others)


def body(tokens, w_query, key_weight, value_weight, segment_ids):
    n_dp = lax.axis_size("dp")
    ring = ring_of(n_dp)
    size = len(ring)
    hops = size // 2
    onward = functools.partial(lax.ppermute, axis_name="dp", perm=ring_pairs(n_dp, 1))
    back = functools.partial(lax.ppermute, axis_name="dp", perm=ring_pairs(n_dp, -1))
    sibling = functools.partial(lax.ppermute, axis_name="dp", perm=[(at, at ^ 1) for at in range(n_dp)])

    table = []
    for device in range(n_dp):
        at, core = ring.index(device // 2), device % 2
        owners = [device, device ^ 1]
        for hop in range(1, hops + 1):
            for step in (hop, -hop)[: 2 if hop < hops else 1]:
                for sender in (core, 1 - core):
                    owners.append(ring[(at - (step if sender == 0 else -step)) % size] * 2 + sender)
        table.append(owners)
    order = jnp.asarray(table, jnp.int32)[lax.axis_index("dp")]

    columns = w_query.shape[1]
    widths = []
    while columns - sum(widths) > 2 * NARROW:
        widths.append(WIDE)
    widths += [NARROW] * ((columns - sum(widths)) // NARROW)
    starts = [sum(widths[:at]) for at in range(len(widths))]
    w_sibling = sibling(w_query)
    own = [jnp.concatenate([key_weight, value_weight], axis=1)]
    own += [w_query[:, at : at + width] for at, width in zip(starts, widths)]
    own_sibling = [sibling(own[0])] + [w_sibling[:, at : at + width] for at, width in zip(starts, widths)]
    last = len(own) - 1
    seg_row = segment_ids.reshape(1, -1)
    seg_col = segment_ids.reshape(-1, 1)

    near = {}
    far = {}
    kv = out = done = None

    def work(chunk):
        nonlocal kv, out, done
        if chunk == 0:
            kv, done = chunk_call(tokens, order, near[0] + far[0], "round", "project_keys_values", done)
            return
        at = chunk - 1
        attention = (kv, starts[at] // (GROUP * HEAD_SIZE), seg_row, seg_col, out, starts[at], columns)
        if chunk < last:
            out, done = chunk_call(
                tokens, order, near[chunk] + far[chunk], "attend", "project_attend", done, None, attention
            )
        else:
            n_near = len(near[chunk])
            start, done = chunk_call(tokens, order[:n_near], near[chunk], "partial", "project_near", done)
            out, done = chunk_call(
                tokens, order[n_near:], far[chunk], "attend", "project_far_attend", done, start, attention
            )

    def exchange(chunk, pieces):
        return onward(pieces[0]), back(pieces[1])

    moving = exchange(0, (own[0], own[0])) if hops > 1 else (own[0],) * 2
    for chunk in range(last + 1):
        arrived = [own[chunk], own_sibling[chunk]]
        for hop in range(1, hops):
            if hop > 1:
                moving = exchange(chunk, moving)
            arrived += [moving[0], None, moving[1], None]
        ahead = own[chunk + 1] if chunk < last else None
        waits = [moving[0], moving[1]] + ([ahead] if ahead is not None else []) + ([done] if done is not None else [])
        held = list(hold(*waits))
        moving = held[:2]
        if ahead is not None:
            ahead = held[2]
        if done is not None:
            done = held[-1]
        if hops > 1:
            arrived[-4], arrived[-2] = moving
        farthest = onward(moving[0])
        if ahead is not None:
            moving = exchange(chunk + 1, (ahead, ahead)) if hops > 1 else (ahead,) * 2
        for at in range(2, len(arrived), 2):
            arrived[at + 1] = sibling(arrived[at])
        near[chunk] = arrived
        if chunk > 0:
            work(chunk - 1)
            farthest, done = hold(farthest, done)
        far[chunk] = [farthest, sibling(farthest)]
    work(last)
    return out


def solution(mesh):
    in_specs = (P("dp", None), P("dp", "head"), P("dp", "head"), P("dp", "head"), P("dp"))
    out_specs = P("dp", "head")
    return jax.shard_map(body, mesh=mesh, in_specs=in_specs, out_specs=out_specs, check_vma=False)
```

```python
import functools
import math

import jax
import jax.numpy as jnp
from jax import lax
from jax.experimental import pallas as pl
from jax.experimental.pallas import tpu as pltpu
from jax.sharding import PartitionSpec as P

QUERY_HEADS = 64
KEY_VALUE_HEADS = 8
HEAD_SIZE = 128
GROUP = QUERY_HEADS // KEY_VALUE_HEADS
ROW_BLOCK = 256
WIDE = 512
NARROW = [256, 256]
NEGATIVE = -1e30
VMEM_BYTES = 16 * 1024 * 1024


def ring_of(n_dp):
    chips = n_dp // 2
    half = chips // 2
    return list(range(half)) + list(range(chips - 1, half - 1, -1))


def ring_pairs(n_dp, step):
    ring = ring_of(n_dp)
    size = len(ring)
    return [
        (ring[at] * 2 + core, ring[(at + (step if core == 0 else -step)) % size] * 2 + core)
        for at in range(size)
        for core in range(2)
    ]


def attend_rows(query, keys, values, allowed):
    scale = math.log2(math.e) / math.sqrt(HEAD_SIZE)
    scores = lax.dot_general(query, keys, (((1,), (1,)), ((), ())), preferred_element_type=jnp.float32)
    scores = jnp.where(allowed, scores, NEGATIVE)
    top = jnp.max(scores, axis=1, keepdims=True)
    weights = jnp.exp2((scores - top) * scale).astype(jnp.bfloat16)
    values = jnp.concatenate([values, jnp.ones_like(values)], axis=1)
    summed = jnp.dot(weights, values, preferred_element_type=jnp.float32)
    return (summed[:, :HEAD_SIZE] / summed[:, HEAD_SIZE:]).astype(jnp.bfloat16)


def chunk_kernel(n_pieces, has_start, mode, column, order_ref, tokens_ref, *refs):
    pieces, refs = refs[:n_pieces], refs[n_pieces:]
    rows = tokens_ref.shape[0]
    depth, width = pieces[0].shape
    total = None
    if has_start:
        total = refs[0][...]
        refs = refs[1:]
    for at, piece in enumerate(pieces):
        columns = pl.ds(pl.multiple_of(order_ref[at] * depth, depth), depth)
        part = jnp.dot(tokens_ref[:, columns], piece[...], preferred_element_type=jnp.float32)
        total = part if total is None else total + part
    if mode == "partial":
        refs[-2][...] = total
        refs[-1][...] = jnp.zeros_like(refs[-1])
        return
    if mode == "round":
        refs[-2][...] = total.astype(jnp.bfloat16)
        refs[-1][...] = jnp.zeros_like(refs[-1])
        return
    kv_ref, seg_row_ref, seg_col_ref = refs[:3]
    out_ref, done_ref, query_ref, block_ref, out_sem = refs[-5:]
    done_ref[...] = jnp.zeros_like(done_ref)
    query_ref[...] = total.astype(jnp.bfloat16)
    half = kv_ref.shape[1] // 2
    for number in range(rows // ROW_BLOCK):
        start, stop = number * ROW_BLOCK, (number + 1) * ROW_BLOCK
        at_q = start + lax.broadcasted_iota(jnp.int32, (ROW_BLOCK, stop), 0)
        at_k = lax.broadcasted_iota(jnp.int32, (ROW_BLOCK, stop), 1)
        allowed = (seg_col_ref[start:stop, :] == seg_row_ref[:, :stop]) & (at_k <= at_q)
        for head in range(0, width, HEAD_SIZE):
            kv_at = (column + head) // (GROUP * HEAD_SIZE) * HEAD_SIZE
            block_ref[start:stop, head : head + HEAD_SIZE] = attend_rows(
                query_ref[start:stop, head : head + HEAD_SIZE],
                kv_ref[:stop, kv_at : kv_at + HEAD_SIZE],
                kv_ref[:stop, half + kv_at : half + kv_at + HEAD_SIZE],
                allowed,
            )
    copy = pltpu.make_async_copy(block_ref, out_ref.at[:, pl.ds(column, width)], out_sem)
    copy.start()
    copy.wait()


def chunk_call(tokens, order, pieces, mode, name, done, start=None, attention=None):
    rows, model = tokens.shape
    depth, width = pieces[0].shape
    in_hbm = pl.BlockSpec(memory_space=pltpu.HBM)
    in_vmem = pl.BlockSpec(memory_space=pltpu.VMEM)
    args = [order, tokens] + list(pieces)
    if start is not None:
        args.append(start)
    in_specs = [pl.BlockSpec(memory_space=pltpu.SMEM)] + [in_vmem] * (len(args) - 1)
    aliases = {}
    scratch = []
    flops = 2 * rows * depth * len(pieces) * width
    column = 0
    out_spec = in_vmem
    out_shape = jax.ShapeDtypeStruct((rows, width), jnp.float32 if mode == "partial" else jnp.bfloat16)
    if mode == "attend":
        kv, seg_row, seg_col, out, column, out_columns = attention
        args += [kv, seg_row, seg_col]
        in_specs += [in_vmem] * 3
        flops += 8 * rows * rows * width
        out_spec = in_hbm
        out_shape = jax.ShapeDtypeStruct((rows, out_columns), jnp.bfloat16)
        scratch = [
            pltpu.VMEM((rows, width), jnp.bfloat16),
            pltpu.VMEM((rows, width), jnp.bfloat16),
            pltpu.SemaphoreType.DMA,
        ]
        if out is not None:
            aliases = {len(args): 0}
            in_specs.append(in_hbm)
            args.append(out)
    if done is not None:
        in_specs.append(in_vmem)
        args.append(done)
    return pl.pallas_call(
        functools.partial(chunk_kernel, len(pieces), start is not None, mode, column),
        in_specs=in_specs,
        out_specs=(out_spec, in_vmem),
        out_shape=(out_shape, jax.ShapeDtypeStruct((8, 128), jnp.float32)),
        scratch_shapes=scratch,
        input_output_aliases=aliases,
        compiler_params=pltpu.CompilerParams(vmem_limit_bytes=VMEM_BYTES),
        cost_estimate=pl.CostEstimate(flops=flops, bytes_accessed=0, transcendentals=0),
        name=name,
    )(*args)


def hold(value, *others):
    return lax.optimization_barrier((value,) + others)


def body(tokens, w_query, key_weight, value_weight, segment_ids):
    n_dp = lax.axis_size("dp")
    ring = ring_of(n_dp)
    size = len(ring)
    hops = size // 2
    onward = functools.partial(lax.ppermute, axis_name="dp", perm=ring_pairs(n_dp, 1))
    back = functools.partial(lax.ppermute, axis_name="dp", perm=ring_pairs(n_dp, -1))
    sibling = functools.partial(lax.ppermute, axis_name="dp", perm=[(at, at ^ 1) for at in range(n_dp)])

    table = []
    for device in range(n_dp):
        at, core = ring.index(device // 2), device % 2
        owners = [device, device ^ 1]
        for hop in range(1, hops + 1):
            for step in (hop, -hop)[: 2 if hop < hops else 1]:
                for sender in (core, 1 - core):
                    owners.append(ring[(at - (step if sender == 0 else -step)) % size] * 2 + sender)
        table.append(owners)
    order = jnp.asarray(table, jnp.int32)[lax.axis_index("dp")]

    columns = w_query.shape[1]
    n_wide = (columns - sum(NARROW)) // WIDE
    widths = [columns - sum(NARROW) - WIDE * (n_wide - 1)] + [WIDE] * (n_wide - 1) + NARROW
    starts = [sum(widths[:at]) for at in range(len(widths))]
    w_sibling = sibling(w_query)
    own = [jnp.concatenate([key_weight, value_weight], axis=1)]
    own += [w_query[:, at : at + width] for at, width in zip(starts, widths)]
    own_sibling = [sibling(own[0])] + [w_sibling[:, at : at + width] for at, width in zip(starts, widths)]
    last = len(own) - 1
    seg_row = segment_ids.reshape(1, -1)
    seg_col = segment_ids.reshape(-1, 1)

    far = {}
    kv = out = done = None

    sums = {}

    def project(chunk, pieces, first):
        nonlocal done
        sums[chunk], done = chunk_call(
            tokens, order[first : first + len(pieces)], pieces, "partial", "project_part", done, sums.get(chunk)
        )

    def work(chunk):
        nonlocal kv, out, done
        late = order[order.shape[0] - 2 :]
        if chunk == 0:
            kv, done = chunk_call(tokens, late, far[0], "round", "project_keys_values", done, sums[0])
        else:
            at = starts[chunk - 1]
            attention = (kv, seg_row, seg_col, out, at, columns)
            out, done = chunk_call(tokens, late, far[chunk], "attend", "project_attend", done, sums[chunk], attention)

    def exchange(chunk, pieces):
        with jax.named_scope(f"near_{chunk}"):
            return onward(pieces[0]), back(pieces[1])

    moving = exchange(0, (own[0], own[0])) if hops > 1 else (own[0],) * 2
    for chunk in range(last + 1):
        arrived = [own[chunk], own_sibling[chunk]]
        for hop in range(1, hops):
            if hop > 1:
                moving = exchange(chunk, moving)
            arrived += [moving[0], None, moving[1], None]
        ahead = own[chunk + 1] if chunk < last else None
        waits = [moving[0], moving[1]] + ([ahead] if ahead is not None else []) + ([done] if done is not None and chunk < last else [])
        if chunk == 0:
            *waits[:2], own, own_sibling = lax.optimization_barrier((*waits[:2], own, own_sibling))
            ahead = own[1]
            waits[2:3] = [ahead]
        held = list(hold(*waits))
        moving = held[:2]
        if ahead is not None:
            ahead = held[2]
        if len(waits) > len(held[:2]) + (ahead is not None):
            done = held[-1]
        if hops > 1:
            arrived[-4], arrived[-2] = moving
        with jax.named_scope(f"far_{chunk}"):
            farthest = onward(moving[0])
        if ahead is not None:
            moving = exchange(chunk + 1, (ahead, ahead)) if hops > 1 else (ahead,) * 2
        for other in range(min(3, last + 1)) if chunk == 0 else range(3, last + 1) if chunk == 1 else ():
            project(other, [own[other], own_sibling[other]], 0)
        for at in range(2, len(arrived), 2):
            with jax.named_scope(f"near_{chunk}_sibling"):
                arrived[at + 1] = sibling(arrived[at])
        if len(arrived) > 2:
            project(chunk, arrived[2:], 2)
        if chunk > 0:
            work(chunk - 1)
        if chunk < last:
            farthest, *moving, done = hold(farthest, *moving, done)
        else:
            farthest, done = hold(farthest, done)
        with jax.named_scope(f"far_{chunk}_sibling"):
            far[chunk] = [farthest, sibling(farthest)]
    work(last)
    return out


def solution(mesh):
    in_specs = (P("dp", None), P("dp", "head"), P("dp", "head"), P("dp", "head"), P("dp"))
    out_specs = P("dp", "head")
    return jax.shard_map(body, mesh=mesh, in_specs=in_specs, out_specs=out_specs, check_vma=False)
```

```python
import functools
import math

import jax
import jax.numpy as jnp
from jax import lax
from jax.experimental import pallas as pl
from jax.experimental.pallas import tpu as pltpu
from jax.sharding import PartitionSpec as P

QUERY_HEADS = 64
KEY_VALUE_HEADS = 8
HEAD_SIZE = 128
GROUP = QUERY_HEADS // KEY_VALUE_HEADS
ROW_BLOCK = 256
WIDE = 512
NARROW = [256, 256]
NEGATIVE = -1e30
VMEM_BYTES = 16 * 1024 * 1024


def ring_of(n_dp):
    chips = n_dp // 2
    half = chips // 2
    return list(range(half)) + list(range(chips - 1, half - 1, -1))


def ring_pairs(n_dp, step):
    ring = ring_of(n_dp)
    size = len(ring)
    return [
        (ring[at] * 2 + core, ring[(at + (step if core == 0 else -step)) % size] * 2 + core)
        for at in range(size)
        for core in range(2)
    ]


def attend_blocks(items):
    scale = math.log2(math.e) / math.sqrt(HEAD_SIZE)
    scores = [
        lax.dot_general(query, keys, (((1,), (1,)), ((), ())), preferred_element_type=jnp.float32)
        for query, keys, _, _ in items
    ]
    scores = [jnp.where(item[3], score, NEGATIVE) for item, score in zip(items, scores)]
    tops = [jnp.max(score, axis=1, keepdims=True) for score in scores]
    weights = [jnp.exp2((score - top) * scale).astype(jnp.bfloat16) for score, top in zip(scores, tops)]
    results = []
    for (_, _, values, _), weight in zip(items, weights):
        values = jnp.concatenate([values, jnp.ones_like(values)], axis=1)
        summed = jnp.dot(weight, values, preferred_element_type=jnp.float32)
        results.append((summed[:, :HEAD_SIZE] / summed[:, HEAD_SIZE:]).astype(jnp.bfloat16))
    return results


def chunk_kernel(n_pieces, has_start, mode, column, order_ref, tokens_ref, *refs):
    pieces, refs = refs[:n_pieces], refs[n_pieces:]
    rows = tokens_ref.shape[0]
    depth, width = pieces[0].shape
    total = None
    if has_start:
        total = refs[0][...]
        refs = refs[1:]
    for at, piece in enumerate(pieces):
        columns = pl.ds(pl.multiple_of(order_ref[at] * depth, depth), depth)
        part = jnp.dot(tokens_ref[:, columns], piece[...], preferred_element_type=jnp.float32)
        total = part if total is None else total + part
    if mode == "partial":
        refs[-2][...] = total
        refs[-1][...] = jnp.zeros_like(refs[-1])
        return
    if mode == "round":
        refs[-2][...] = total.astype(jnp.bfloat16)
        refs[-1][...] = jnp.zeros_like(refs[-1])
        return
    kv_ref, seg_row_ref, seg_col_ref = refs[:3]
    out_ref, done_ref, query_ref, block_ref, out_sems = refs[-5:]
    done_ref[...] = jnp.zeros_like(done_ref)
    query_ref[...] = total.astype(jnp.bfloat16)
    half = kv_ref.shape[1] // 2
    n_blocks = rows // ROW_BLOCK
    copies = []
    for first in range((n_blocks + 1) // 2):
        numbers = sorted({first, n_blocks - 1 - first})
        items, places = [], []
        for number in numbers:
            start, stop = number * ROW_BLOCK, (number + 1) * ROW_BLOCK
            at_q = start + lax.broadcasted_iota(jnp.int32, (ROW_BLOCK, stop), 0)
            at_k = lax.broadcasted_iota(jnp.int32, (ROW_BLOCK, stop), 1)
            allowed = (seg_col_ref[start:stop, :] == seg_row_ref[:, :stop]) & (at_k <= at_q)
            for head in range(0, width, HEAD_SIZE):
                kv_at = (column + head) // (GROUP * HEAD_SIZE) * HEAD_SIZE
                items.append(
                    (
                        query_ref[start:stop, head : head + HEAD_SIZE],
                        kv_ref[:stop, kv_at : kv_at + HEAD_SIZE],
                        kv_ref[:stop, half + kv_at : half + kv_at + HEAD_SIZE],
                        allowed,
                    )
                )
                places.append((start, stop, head))
        for (start, stop, head), result in zip(places, attend_blocks(items)):
            block_ref[start:stop, head : head + HEAD_SIZE] = result
        for number in numbers:
            block = pl.ds(number * ROW_BLOCK, ROW_BLOCK)
            copy = pltpu.make_async_copy(
                block_ref.at[block, :], out_ref.at[block, pl.ds(column, width)], out_sems.at[number]
            )
            copy.start()
            copies.append(copy)
    for copy in copies:
        copy.wait()


def chunk_call(tokens, order, pieces, mode, name, done, start=None, attention=None):
    rows, model = tokens.shape
    depth, width = pieces[0].shape
    in_hbm = pl.BlockSpec(memory_space=pltpu.HBM)
    in_vmem = pl.BlockSpec(memory_space=pltpu.VMEM)
    args = [order, tokens] + list(pieces)
    if start is not None:
        args.append(start)
    in_specs = [pl.BlockSpec(memory_space=pltpu.SMEM)] + [in_vmem] * (len(args) - 1)
    aliases = {}
    scratch = []
    flops = 2 * rows * depth * len(pieces) * width
    column = 0
    out_spec = in_vmem
    out_shape = jax.ShapeDtypeStruct((rows, width), jnp.float32 if mode == "partial" else jnp.bfloat16)
    if mode == "attend":
        kv, seg_row, seg_col, out, column, out_columns = attention
        args += [kv, seg_row, seg_col]
        in_specs += [in_vmem] * 3
        flops += 8 * rows * rows * width
        out_spec = in_hbm
        out_shape = jax.ShapeDtypeStruct((rows, out_columns), jnp.bfloat16)
        scratch = [
            pltpu.VMEM((rows, width), jnp.bfloat16),
            pltpu.VMEM((rows, width), jnp.bfloat16),
            pltpu.SemaphoreType.DMA((rows // ROW_BLOCK,)),
        ]
        if out is not None:
            aliases = {len(args): 0}
            in_specs.append(in_hbm)
            args.append(out)
    if done is not None:
        in_specs.append(in_vmem)
        args.append(done)
    return pl.pallas_call(
        functools.partial(chunk_kernel, len(pieces), start is not None, mode, column),
        in_specs=in_specs,
        out_specs=(out_spec, in_vmem),
        out_shape=(out_shape, jax.ShapeDtypeStruct((8, 128), jnp.float32)),
        scratch_shapes=scratch,
        input_output_aliases=aliases,
        compiler_params=pltpu.CompilerParams(vmem_limit_bytes=VMEM_BYTES),
        cost_estimate=pl.CostEstimate(flops=flops, bytes_accessed=0, transcendentals=0),
        name=name,
    )(*args)


def hold(value, *others):
    return lax.optimization_barrier((value,) + others)


def body(tokens, w_query, key_weight, value_weight, segment_ids):
    n_dp = lax.axis_size("dp")
    ring = ring_of(n_dp)
    size = len(ring)
    hops = size // 2
    onward = functools.partial(lax.ppermute, axis_name="dp", perm=ring_pairs(n_dp, 1))
    back = functools.partial(lax.ppermute, axis_name="dp", perm=ring_pairs(n_dp, -1))
    sibling = functools.partial(lax.ppermute, axis_name="dp", perm=[(at, at ^ 1) for at in range(n_dp)])

    table = []
    for device in range(n_dp):
        at, core = ring.index(device // 2), device % 2
        owners = [device, device ^ 1]
        for hop in range(1, hops + 1):
            for step in (hop, -hop)[: 2 if hop < hops else 1]:
                for sender in (core, 1 - core):
                    owners.append(ring[(at - (step if sender == 0 else -step)) % size] * 2 + sender)
        table.append(owners)
    order = jnp.asarray(table, jnp.int32)[lax.axis_index("dp")]

    columns = w_query.shape[1]
    n_wide = (columns - sum(NARROW)) // WIDE
    widths = [columns - sum(NARROW) - WIDE * (n_wide - 1)] + [WIDE] * (n_wide - 1) + NARROW
    starts = [sum(widths[:at]) for at in range(len(widths))]
    w_sibling = sibling(w_query)
    own = [jnp.concatenate([key_weight, value_weight], axis=1)]
    own += [w_query[:, at : at + width] for at, width in zip(starts, widths)]
    own_sibling = [sibling(own[0])] + [w_sibling[:, at : at + width] for at, width in zip(starts, widths)]
    last = len(own) - 1
    seg_row = segment_ids.reshape(1, -1)
    seg_col = segment_ids.reshape(-1, 1)

    far = {}
    kv = out = done = None

    sums = {}

    def project(chunk, pieces, first):
        nonlocal done
        sums[chunk], done = chunk_call(
            tokens, order[first : first + len(pieces)], pieces, "partial", "project_part", done, sums.get(chunk)
        )

    def work(chunk):
        nonlocal kv, out, done
        late = order[order.shape[0] - 2 :]
        if chunk == 0:
            kv, done = chunk_call(tokens, late, far[0], "round", "project_keys_values", done, sums[0])
        else:
            at = starts[chunk - 1]
            attention = (kv, seg_row, seg_col, out, at, columns)
            out, done = chunk_call(tokens, late, far[chunk], "attend", "project_attend", done, sums[chunk], attention)

    def exchange(chunk, pieces):
        with jax.named_scope(f"near_{chunk}"):
            return onward(pieces[0]), back(pieces[1])

    moving = exchange(0, (own[0], own[0])) if hops > 1 else (own[0],) * 2
    for chunk in range(last + 1):
        arrived = [own[chunk], own_sibling[chunk]]
        for hop in range(1, hops):
            if hop > 1:
                moving = exchange(chunk, moving)
            arrived += [moving[0], None, moving[1], None]
        ahead = own[chunk + 1] if chunk < last else None
        waits = [moving[0], moving[1]] + ([ahead] if ahead is not None else []) + ([done] if done is not None and chunk < last else [])
        if chunk == 0:
            *waits[:2], own, own_sibling = lax.optimization_barrier((*waits[:2], own, own_sibling))
            ahead = own[1]
            waits[2:3] = [ahead]
        held = list(hold(*waits))
        moving = held[:2]
        if ahead is not None:
            ahead = held[2]
        if len(waits) > len(held[:2]) + (ahead is not None):
            done = held[-1]
        if hops > 1:
            arrived[-4], arrived[-2] = moving
        with jax.named_scope(f"far_{chunk}"):
            farthest = onward(moving[0])
        if ahead is not None:
            moving = exchange(chunk + 1, (ahead, ahead)) if hops > 1 else (ahead,) * 2
        for other in range(min(3, last + 1)) if chunk == 0 else range(3, last + 1) if chunk == 1 else ():
            project(other, [own[other], own_sibling[other]], 0)
        for at in range(2, len(arrived), 2):
            with jax.named_scope(f"near_{chunk}_sibling"):
                arrived[at + 1] = sibling(arrived[at])
        if chunk < last and hops > 1:
            project(chunk, arrived[2:], 2)
        if chunk > 0:
            work(chunk - 1)
        if chunk < last:
            farthest, *moving, done = hold(farthest, *moving, done)
        else:
            farthest, done = hold(farthest, done)
        with jax.named_scope(f"far_{chunk}_sibling"):
            far[chunk] = [farthest, sibling(farthest)]
    if hops > 1:
        project(last, arrived[2:], 2)
    work(last)
    return out


def solution(mesh):
    in_specs = (P("dp", None), P("dp", "head"), P("dp", "head"), P("dp", "head"), P("dp"))
    out_specs = P("dp", "head")
    return jax.shard_map(body, mesh=mesh, in_specs=in_specs, out_specs=out_specs, check_vma=False)
```

```python
import functools
import math

import jax
import jax.numpy as jnp
from jax import lax
from jax.experimental import pallas as pl
from jax.experimental.pallas import tpu as pltpu
from jax.sharding import PartitionSpec as P

QUERY_HEADS = 64
KEY_VALUE_HEADS = 8
HEAD_SIZE = 128
GROUP = QUERY_HEADS // KEY_VALUE_HEADS
ROW_BLOCK = 256
WIDE = 512
NARROW = [256, 256]
NEGATIVE = -1e30
VMEM_BYTES = 16 * 1024 * 1024


def ring_of(n_dp):
    chips = n_dp // 2
    half = chips // 2
    return list(range(half)) + list(range(chips - 1, half - 1, -1))


def ring_pairs(n_dp, step):
    ring = ring_of(n_dp)
    size = len(ring)
    return [
        (ring[at] * 2 + core, ring[(at + (step if core == 0 else -step)) % size] * 2 + core)
        for at in range(size)
        for core in range(2)
    ]


def attend_blocks(items):
    scale = math.log2(math.e) / math.sqrt(HEAD_SIZE)
    scores = [
        lax.dot_general(query, keys, (((1,), (1,)), ((), ())), preferred_element_type=jnp.float32)
        for query, keys, _, _ in items
    ]
    scores = [jnp.where(item[3], score, NEGATIVE) for item, score in zip(items, scores)]
    tops = [jnp.max(score, axis=1, keepdims=True) for score in scores]
    weights = [jnp.exp2((score - top) * scale).astype(jnp.bfloat16) for score, top in zip(scores, tops)]
    results = []
    for (_, _, values, _), weight in zip(items, weights):
        values = jnp.concatenate([values, jnp.ones_like(values)], axis=1)
        summed = jnp.dot(weight, values, preferred_element_type=jnp.float32)
        results.append((summed[:, :HEAD_SIZE] / summed[:, HEAD_SIZE:]).astype(jnp.bfloat16))
    return results


def join_kernel(left_ref, right_ref, out_ref, sems):
    width = left_ref.shape[1]
    copies = [
        pltpu.make_async_copy(ref, out_ref.at[:, pl.ds(at * width, width)], sems.at[at])
        for at, ref in enumerate((left_ref, right_ref))
    ]
    for copy in copies:
        copy.start()
    for copy in copies:
        copy.wait()


def join(left, right):
    return pl.pallas_call(
        join_kernel,
        in_specs=[pl.BlockSpec(memory_space=pltpu.HBM)] * 2,
        out_specs=pl.BlockSpec(memory_space=pltpu.VMEM),
        out_shape=jax.ShapeDtypeStruct((left.shape[0], 2 * left.shape[1]), left.dtype),
        scratch_shapes=[pltpu.SemaphoreType.DMA((2,))],
        compiler_params=pltpu.CompilerParams(vmem_limit_bytes=VMEM_BYTES),
        name="join_weights",
    )(*(pltpu.with_memory_space_constraint(array, pltpu.HBM) for array in (left, right)))


def chunk_kernel(n_pieces, has_start, mode, column, order_ref, tokens_ref, *refs):
    pieces, refs = refs[:n_pieces], refs[n_pieces:]
    rows = tokens_ref.shape[0]
    depth, width = pieces[0].shape
    total = None
    if has_start:
        total = refs[0][...]
        refs = refs[1:]
    for at, piece in enumerate(pieces):
        columns = pl.ds(pl.multiple_of(order_ref[at] * depth, depth), depth)
        part = jnp.dot(tokens_ref[:, columns], piece[...], preferred_element_type=jnp.float32)
        total = part if total is None else total + part
    if mode == "partial":
        refs[-2][...] = total
        refs[-1][...] = jnp.zeros_like(refs[-1])
        return
    if mode == "round":
        refs[-2][...] = total.astype(jnp.bfloat16)
        refs[-1][...] = jnp.zeros_like(refs[-1])
        return
    kv_ref, seg_row_ref, seg_col_ref = refs[:3]
    out_ref, done_ref, query_ref, block_ref, out_sems = refs[-5:]
    done_ref[...] = jnp.zeros_like(done_ref)
    query_ref[...] = total.astype(jnp.bfloat16)
    half = kv_ref.shape[1] // 2
    n_blocks = rows // ROW_BLOCK
    copies = []
    for first in range((n_blocks + 1) // 2):
        numbers = sorted({first, n_blocks - 1 - first})
        items, places = [], []
        for number in numbers:
            start, stop = number * ROW_BLOCK, (number + 1) * ROW_BLOCK
            at_q = start + lax.broadcasted_iota(jnp.int32, (ROW_BLOCK, stop), 0)
            at_k = lax.broadcasted_iota(jnp.int32, (ROW_BLOCK, stop), 1)
            allowed = (seg_col_ref[start:stop, :] == seg_row_ref[:, :stop]) & (at_k <= at_q)
            for head in range(0, width, HEAD_SIZE):
                kv_at = (column + head) // (GROUP * HEAD_SIZE) * HEAD_SIZE
                items.append(
                    (
                        query_ref[start:stop, head : head + HEAD_SIZE],
                        kv_ref[:stop, kv_at : kv_at + HEAD_SIZE],
                        kv_ref[:stop, half + kv_at : half + kv_at + HEAD_SIZE],
                        allowed,
                    )
                )
                places.append((start, stop, head))
        for (start, stop, head), result in zip(places, attend_blocks(items)):
            block_ref[start:stop, head : head + HEAD_SIZE] = result
        for number in numbers:
            block = pl.ds(number * ROW_BLOCK, ROW_BLOCK)
            copy = pltpu.make_async_copy(
                block_ref.at[block, :], out_ref.at[block, pl.ds(column, width)], out_sems.at[number]
            )
            copy.start()
            copies.append(copy)
    for copy in copies:
        copy.wait()


def chunk_call(tokens, order, pieces, mode, name, done, start=None, attention=None):
    rows, model = tokens.shape
    depth, width = pieces[0].shape
    in_hbm = pl.BlockSpec(memory_space=pltpu.HBM)
    in_vmem = pl.BlockSpec(memory_space=pltpu.VMEM)
    args = [order, tokens] + list(pieces)
    if start is not None:
        args.append(start)
    in_specs = [pl.BlockSpec(memory_space=pltpu.SMEM)] + [in_vmem] * (len(args) - 1)
    aliases = {}
    scratch = []
    flops = 2 * rows * depth * len(pieces) * width
    column = 0
    out_spec = in_vmem
    out_shape = jax.ShapeDtypeStruct((rows, width), jnp.float32 if mode == "partial" else jnp.bfloat16)
    if mode == "attend":
        kv, seg_row, seg_col, out, column, out_columns = attention
        args += [kv, seg_row, seg_col]
        in_specs += [in_vmem] * 3
        flops += 8 * rows * rows * width
        out_spec = in_hbm
        out_shape = jax.ShapeDtypeStruct((rows, out_columns), jnp.bfloat16)
        scratch = [
            pltpu.VMEM((rows, width), jnp.bfloat16),
            pltpu.VMEM((rows, width), jnp.bfloat16),
            pltpu.SemaphoreType.DMA((rows // ROW_BLOCK,)),
        ]
        if out is not None:
            aliases = {len(args): 0}
            in_specs.append(in_hbm)
            args.append(out)
    if done is not None:
        in_specs.append(in_vmem)
        args.append(done)
    return pl.pallas_call(
        functools.partial(chunk_kernel, len(pieces), start is not None, mode, column),
        in_specs=in_specs,
        out_specs=(out_spec, in_vmem),
        out_shape=(out_shape, jax.ShapeDtypeStruct((8, 128), jnp.float32)),
        scratch_shapes=scratch,
        input_output_aliases=aliases,
        compiler_params=pltpu.CompilerParams(vmem_limit_bytes=VMEM_BYTES),
        cost_estimate=pl.CostEstimate(flops=flops, bytes_accessed=0, transcendentals=0),
        name=name,
    )(*args)


def hold(value, *others):
    return lax.optimization_barrier((value,) + others)


def body(tokens, w_query, key_weight, value_weight, segment_ids):
    n_dp = lax.axis_size("dp")
    ring = ring_of(n_dp)
    size = len(ring)
    hops = size // 2
    onward = functools.partial(lax.ppermute, axis_name="dp", perm=ring_pairs(n_dp, 1))
    back = functools.partial(lax.ppermute, axis_name="dp", perm=ring_pairs(n_dp, -1))
    sibling = functools.partial(lax.ppermute, axis_name="dp", perm=[(at, at ^ 1) for at in range(n_dp)])

    table = []
    for device in range(n_dp):
        at, core = ring.index(device // 2), device % 2
        owners = [device, device ^ 1]
        for hop in range(1, hops + 1):
            for step in (hop, -hop)[: 2 if hop < hops else 1]:
                for sender in (core, 1 - core):
                    owners.append(ring[(at - (step if sender == 0 else -step)) % size] * 2 + sender)
        table.append(owners)
    order = jnp.asarray(table, jnp.int32)[lax.axis_index("dp")]

    columns = w_query.shape[1]
    n_wide = (columns - sum(NARROW)) // WIDE
    widths = [columns - sum(NARROW) - WIDE * (n_wide - 1)] + [WIDE] * (n_wide - 1) + NARROW
    starts = [sum(widths[:at]) for at in range(len(widths))]
    w_held, kv_weight = hold(w_query, join(key_weight, value_weight))
    w_sibling = sibling(w_held)
    own = [kv_weight]
    own += [w_query[:, at : at + width] for at, width in zip(starts, widths)]
    own_sibling = [sibling(own[0])] + [w_sibling[:, at : at + width] for at, width in zip(starts, widths)]
    last = len(own) - 1
    seg_row = segment_ids.reshape(1, -1)
    seg_col = segment_ids.reshape(-1, 1)

    far = {}
    kv = out = done = None

    sums = {}

    def project(chunk, pieces, first):
        nonlocal done
        sums[chunk], done = chunk_call(
            tokens, order[first : first + len(pieces)], pieces, "partial", "project_part", done, sums.get(chunk)
        )

    def work(chunk):
        nonlocal kv, out, done
        late = order[order.shape[0] - 2 :]
        if chunk == 0:
            kv, done = chunk_call(tokens, late, far[0], "round", "project_keys_values", done, sums[0])
        else:
            at = starts[chunk - 1]
            attention = (kv, seg_row, seg_col, out, at, columns)
            out, done = chunk_call(tokens, late, far[chunk], "attend", "project_attend", done, sums[chunk], attention)

    def exchange(chunk, pieces):
        with jax.named_scope(f"near_{chunk}"):
            return onward(pieces[0]), back(pieces[1])

    moving = exchange(0, (own[0], own[0])) if hops > 1 else (own[0],) * 2
    for chunk in range(last + 1):
        arrived = [own[chunk], own_sibling[chunk]]
        for hop in range(1, hops):
            if hop > 1:
                moving = exchange(chunk, moving)
            arrived += [moving[0], None, moving[1], None]
        ahead = own[chunk + 1] if chunk < last else None
        waits = [moving[0], moving[1]] + ([ahead] if ahead is not None else []) + ([done] if done is not None and chunk < last else [])
        if chunk == 0:
            *waits[:2], own, own_sibling = lax.optimization_barrier((*waits[:2], own, own_sibling))
            ahead = own[1]
            waits[2:3] = [ahead]
        held = list(hold(*waits))
        moving = held[:2]
        if ahead is not None:
            ahead = held[2]
        if len(waits) > len(held[:2]) + (ahead is not None):
            done = held[-1]
        if hops > 1:
            arrived[-4], arrived[-2] = moving
        with jax.named_scope(f"far_{chunk}"):
            farthest = onward(moving[0])
        if ahead is not None:
            moving = exchange(chunk + 1, (ahead, ahead)) if hops > 1 else (ahead,) * 2
        for other in range(min(3, last + 1)) if chunk == 0 else range(3, last + 1) if chunk == 1 else ():
            project(other, [own[other], own_sibling[other]], 0)
        for at in range(2, len(arrived), 2):
            with jax.named_scope(f"near_{chunk}_sibling"):
                arrived[at + 1] = sibling(arrived[at])
        if chunk < last and hops > 1:
            project(chunk, arrived[2:], 2)
        if chunk > 0:
            work(chunk - 1)
        if chunk < last:
            farthest, *moving, done = hold(farthest, *moving, done)
        else:
            farthest, done = hold(farthest, done)
        with jax.named_scope(f"far_{chunk}_sibling"):
            far[chunk] = [farthest, sibling(farthest)]
    if hops > 1:
        project(last, arrived[2:], 2)
    work(last)
    return out


def solution(mesh):
    in_specs = (P("dp", None), P("dp", "head"), P("dp", "head"), P("dp", "head"), P("dp"))
    out_specs = P("dp", "head")
    return jax.shard_map(body, mesh=mesh, in_specs=in_specs, out_specs=out_specs, check_vma=False)
```
